512 devices in a mesh: mode: 4 (over x), tm: 16 (over z, core), gz: 8 (over y).
Axes of the slice: x: 4, y: 8, z: 8, core: 2. Of those that a mesh axis runs over, the one named last changes fastest.
Arguments:
- vectors: bfloat16 [32, 2, 12, 262144], P('mode', None, None, ('tm', 'gz')), may hold values from -0.0024414062 to 0.0024414062
- sources: bfloat16 [12, 2, 12, 262144], P(None, None, None, ('tm', 'gz')), may hold values from -6 to 6
- eigenvalues: float32 [32], replicated, may hold values from 0.00159472 to 0.015947198
Outputs:
- guesses: float32 [12, 2, 12, 262144], P('mode', None, None, ('tm', 'gz'))
The draws below stay inside these ranges and needn't reach their ends.
All inputs are finite; a program needn't handle non-finite values.
Results may differ from the reference program's by a relative error of at most 0.0035.
Values may be sent and summed in bfloat16 or wider, within the bound.
A program may use at most 64 MiB of HBM per device.

```python
import math
import jax
import jax.numpy as jnp
from jax import lax

MODES = 32
NSRC = 12
COMP = 12
SITES = 262144


def steps_of(stream_key, shape, shards, smallest, largest):
    factor_of, own = 1.0, jax.random.fold_in(stream_key, 6)
    for dim, shards_of in shards:
        steps = jnp.exp(jax.random.uniform(jax.random.fold_in(own, dim), (shards_of,), jnp.float32, smallest / len(shards), largest / len(shards)))
        factor_of = factor_of * jnp.repeat(steps, shape[dim] // shards_of).reshape([-1 if axis == dim else 1 for axis in range(len(shape))])
    return factor_of


def bell_draw(key, shape, deviation, bound, cuts=(), kind=jnp.bfloat16):
    values = deviation * jax.random.normal(key, shape, jnp.float32)
    if cuts:
        values = values * steps_of(key, shape, cuts, -0.22, 0.18)
    return jnp.clip(values, -bound, bound).astype(kind)


def setup_inputs(seed: int = 0) -> dict:
    keys = jax.random.split(jax.random.key(seed), 4)
    vectors = bell_draw(keys[0], (MODES, 2, COMP, SITES), (24 * SITES) ** -0.5, 0.0024414062, ((0, 4), (3, 128)))
    sources = bell_draw(keys[1], (NSRC, 2, COMP, SITES), 1.0, 6.0, ((3, 128),))
    eigenvalues = jnp.clip(jnp.exp(jax.random.uniform(keys[2], (MODES,), jnp.float32, math.log(0.00159472), math.log(0.015947198))), 0.00159472, 0.015947198)
    return dict(vectors=vectors, sources=sources, eigenvalues=eigenvalues)


def contract_last(left, right):
    return lax.dot_general(left, right, (((1,), (1,)), ((), ())), preferred_element_type=jnp.float32)


def contract_first(left, right):
    return lax.dot_general(left, right, (((0,), (0,)), ((), ())), preferred_element_type=jnp.float32)


def reference(vectors, sources, eigenvalues):
    mode_count = vectors.shape[0]
    src_count = sources.shape[0]
    real_vec = vectors[:, 0].reshape(mode_count, -1)
    imag_vec = vectors[:, 1].reshape(mode_count, -1)
    real_src = sources[:, 0].reshape(src_count, -1)
    imag_src = sources[:, 1].reshape(src_count, -1)
    coef_real = contract_last(real_vec, real_src) + contract_last(imag_vec, imag_src)
    coef_imag = contract_last(real_vec, imag_src) - contract_last(imag_vec, real_src)
    scale_real = (coef_real / eigenvalues[:, None]).astype(jnp.bfloat16)
    scale_imag = (coef_imag / eigenvalues[:, None]).astype(jnp.bfloat16)
    guess_real = contract_first(scale_real, real_vec) - contract_first(scale_imag, imag_vec)
    guess_imag = contract_first(scale_imag, real_vec) + contract_first(scale_real, imag_vec)
    return jnp.stack([guess_real, guess_imag], 1).reshape(src_count, 2, COMP, SITES)
```

```python
import functools

import jax
import jax.numpy as jnp
from jax import lax
from jax.experimental import pallas as pl
from jax.experimental.pallas import tpu as pltpu
from jax.sharding import PartitionSpec as P

MESH = pl.DeviceIdType.MESH
F32, BF16 = jnp.float32, jnp.bfloat16
K, S, C, T = 8, 12, 12, 16
HALF = C // 2
VROWS, SROWS = K * 2 * T, S * 2 * T
OUT = 3


def iota(shape, dim):
    return lax.broadcasted_iota(jnp.int32, shape, dim)


def places():
    m, t, g = lax.axis_index("mode"), lax.axis_index("tm"), lax.axis_index("gz")
    near = m + 1 - 2 * lax.rem(m, 2)
    far = 3 - m
    return m, t, g, near, far


def plane_peers():
    m, t, g, _, _ = places()
    other = t + 1 - 2 * lax.rem(t, 2)
    peers = []
    for j in (4, 3, 5, 2, 6, 1, 7, 0):
        gz = lax.rem(g + j, 8)
        peers.append((m, other, gz))
        if j:
            peers.append((m, t, gz))
    return peers


def line_peers():
    m, t, g, near, far = places()
    peers = []
    for j in (4, 3, 5, 2, 6, 1, 7, 0):
        tm = lax.rem(t + 2 * j, 16)
        peers.append(((near, tm, g), 1))
        peers.append(((far, tm, g), 2))
        if j:
            peers.append(((m, tm, g), 0))
    return peers


def split3(x):
    high = x.astype(BF16)
    rest = x - high.astype(F32)
    mid = rest.astype(BF16)
    low = (rest - mid.astype(F32)).astype(BF16)
    return jnp.concatenate([high, mid, low], axis=0)


def same_tile():
    return (iota((32, VROWS), 0) // 2 == (iota((32, VROWS), 1) // 2) % T).astype(F32)


def partial_coefs(v, b):
    left = jnp.concatenate([b[:, c].reshape(SROWS, 128) for c in range(C)], axis=1)
    right = jnp.concatenate([v[:, c].reshape(VROWS, 128) for c in range(C)], axis=1)
    gram = lax.dot_general(left, right, (((1,), (1,)), ((), ())), preferred_element_type=F32)
    gram = gram.reshape(S, 32, VROWS) * same_tile()[None]
    x = gram.reshape(S, 4, 8, VROWS).sum(axis=1)
    x = x + pltpu.roll(x, 4, 1)
    x = x + pltpu.roll(x, 2, 1)
    sub = iota((8, VROWS), 0) // 2
    blocks = []
    for q in range(3):
        y = jnp.zeros((8, VROWS), F32)
        for i in range(4):
            y = jnp.where(sub == i, x[4 * q + i], y)
        blocks.append(y)
    y = split3(jnp.concatenate(blocks, axis=1))
    row, lane = iota((3 * VROWS, 128), 0), iota((3 * VROWS, 128), 1)
    pick = (lane == (row // VROWS) * 16 + ((row // 32) % K) * 2 + row % 2).astype(BF16)
    z = jnp.dot(y, pick, preferred_element_type=F32)
    return z[0:8] + z[8:16] + z[16:24]


def weights_of(sums, e_ref, modes, targets):
    sub, lane = iota((8, 128), 0), iota((8, 128), 1)
    rows = []
    for total, mode in zip(sums, modes):
        other = jnp.where(sub % 2 == 1, pltpu.roll(total, 1, 0), pltpu.roll(total, 7, 0))
        other = jnp.where(lane % 2 == 1, pltpu.roll(other, 1, 1), pltpu.roll(other, 127, 1))
        coef = total + jnp.where(sub % 2 == lane % 2, other, -other)
        eig = jnp.ones((8, 128), F32)
        for k in range(K):
            eig = jnp.where((lane // 2) % K == k, e_ref[mode * K + k], eig)
        rows.append((coef / eig).astype(BF16))
    small = jnp.concatenate(rows, axis=0)
    row, col = iota((128, 3 * VROWS), 0), iota((128, 3 * VROWS), 1)
    spread = (row == (col // VROWS) * 16 + ((col // 32) % K) * 2 + col % 2).astype(BF16)
    wide = jnp.dot(small, spread, preferred_element_type=F32)
    wide = jnp.concatenate(
        [
            jnp.concatenate([wide[8 * g : 8 * g + 8, q * VROWS : (q + 1) * VROWS] for q in range(3)], axis=0)
            for g in range(3)
        ],
        axis=1,
    ).astype(BF16)
    shape = (3 * 32 * OUT, 24)
    row, col = iota(shape, 0), iota(shape, 1)
    target = jnp.where(row < 32 * OUT, targets[0], jnp.where(row < 64 * OUT, targets[1], targets[2]))
    source = target * OUT + (row // 32) % OUT
    choose = (col == source * 2 + row % 2).astype(BF16)
    full = jnp.dot(choose, wide, preferred_element_type=F32)
    tile = same_tile()
    full = full.reshape(3 * OUT, 32, 3 * VROWS) * jnp.concatenate([tile] * 3, axis=1)[None]
    return full.reshape(3 * 32 * OUT, 3 * VROWS).astype(BF16)


def kernel(
    v_hbm, b_hbm, e_ref, o_ref,
    v, b, pair, first, slots1, second, slots2, send, recv,
    load_sem, pair_send, pair_recv, send1, recv1, send2, recv2, send3, recv3,
):
    m, t, g, near, far = places()
    core, z = lax.rem(t, 2), t // 2
    load_v = pltpu.make_async_copy(v_hbm, v, load_sem.at[0])
    load_b = pltpu.make_async_copy(b_hbm, b, load_sem.at[1])
    load_v.start()
    load_b.start()

    plane, line = plane_peers(), line_peers()
    barrier = pltpu.get_barrier_semaphore()
    for peer in plane + [p for p, _ in line]:
        pl.semaphore_signal(barrier, inc=1, device_id=peer, device_id_type=MESH)
    pl.semaphore_wait(barrier, len(plane) + len(line))

    load_v.wait()
    beside = ((near, t, g), (far, t, g))
    exchange = []
    for h in range(2):
        copy = pltpu.make_async_remote_copy(
            v.at[:, pl.ds(h * HALF, HALF)], pair.at[h], pair_send.at[h], pair_recv.at[h],
            device_id=beside[h], device_id_type=MESH,
        )
        copy.start()
        exchange.append(copy)
    load_b.wait()

    mine = partial_coefs(v, b)
    first[...] = mine
    own = g * 2 + core
    for peer in plane:
        pltpu.make_async_remote_copy(
            first, slots1.at[own], send1, recv1, device_id=peer, device_id_type=MESH
        ).start()
    slots1[own] = mine
    got = slots1.at[pl.ds(0, len(plane))]
    pltpu.make_async_copy(got, got, recv1).wait()
    total = slots1[...].sum(axis=0)

    second[...] = total
    for peer, group in line:
        pltpu.make_async_remote_copy(
            second, slots2.at[group * 8 + z], send2, recv2, device_id=peer, device_id_type=MESH
        ).start()
    slots2[z] = total
    got2 = slots2.at[pl.ds(0, len(line))]
    pltpu.make_async_copy(got2, got2, recv2).wait()
    sums = [slots2[8 * i : 8 * i + 8].sum(axis=0) for i in range(3)]

    w = weights_of(sums, e_ref, (m, near, far), (m, near, far))
    R = 32 * OUT
    sends = []
    for h in range(2):
        exchange[h].wait_recv()
        mate, dest = (1, 2) if h == 0 else (2, 1)
        left = jnp.concatenate(
            [
                jnp.concatenate([w[d * R : d * R + R, k * VROWS : (k + 1) * VROWS] for k in (0, mate)], axis=1)
                for d in (0, dest)
            ],
            axis=0,
        )
        right = jnp.concatenate(
            [
                jnp.concatenate([ref[:, c0 + c].reshape(VROWS, 128) for c in range(HALF)], axis=1)
                for ref, c0 in ((v, h * HALF), (pair.at[h], 0))
            ],
            axis=0,
        )
        out = jnp.dot(left, right, preferred_element_type=F32)
        for c in range(HALF):
            part = out[:, c * 128 : c * 128 + 128]
            o_ref[:, h * HALF + c] = part[:R].reshape(OUT, 32, 128)
            send[h, :, c] = part[R:].astype(BF16).reshape(OUT, 32, 128)
        copy = pltpu.make_async_remote_copy(
            send.at[h], recv.at[h], send3.at[h], recv3.at[h],
            device_id=beside[1 - h], device_id_type=MESH,
        )
        copy.start()
        sends.append(copy)
    for h in range(2):
        sends[h].wait_recv()
        o_ref[:, h * HALF : (h + 1) * HALF] += recv[h].astype(F32)

    for h in range(2):
        exchange[h].wait_send()
        sends[h].wait_send()
    pltpu.make_async_copy(got, got, send1).wait()
    pltpu.make_async_copy(got2, got2, send2).wait()


def on_device(vectors, sources, eigenvalues):
    def tiles(x):
        n = x.shape[0]
        return x.reshape(n, 2, C, T, 128).transpose(0, 2, 3, 1, 4).reshape(n, C, 2 * T, 128)

    dma = pltpu.SemaphoreType.DMA
    out = pl.pallas_call(
        kernel,
        out_shape=jax.ShapeDtypeStruct((OUT, C, 2 * T, 128), F32),
        in_specs=[
            pl.BlockSpec(memory_space=pltpu.HBM),
            pl.BlockSpec(memory_space=pltpu.HBM),
            pl.BlockSpec(memory_space=pltpu.SMEM),
        ],
        out_specs=pl.BlockSpec(memory_space=pltpu.VMEM),
        scratch_shapes=[
            pltpu.VMEM((K, C, 2 * T, 128), BF16),
            pltpu.VMEM((S, C, 2 * T, 128), BF16),
            pltpu.VMEM((2, K, HALF, 2 * T, 128), BF16),
            pltpu.VMEM((8, 128), F32),
            pltpu.VMEM((16, 8, 128), F32),
            pltpu.VMEM((8, 128), F32),
            pltpu.VMEM((24, 8, 128), F32),
            pltpu.VMEM((2, OUT, HALF, 2 * T, 128), BF16),
            pltpu.VMEM((2, OUT, HALF, 2 * T, 128), BF16),
            dma((2,)), dma((2,)), dma((2,)), dma, dma, dma, dma, dma((2,)), dma((2,)),
        ],
        compiler_params=pltpu.CompilerParams(
            collective_id=0, has_side_effects=True, vmem_limit_bytes=60 * 2**20
        ),
        name="deflate",
    )(tiles(vectors), tiles(sources), eigenvalues)
    return out.reshape(OUT, C, T, 2, 128).transpose(0, 3, 1, 2, 4).reshape(OUT, 2, C, T * 128)


def solution(mesh):
    in_specs = (P("mode", None, None, ("tm", "gz")), P(None, None, None, ("tm", "gz")), P())
    out_specs = P("mode", None, None, ("tm", "gz"))
    return jax.shard_map(
        on_device, mesh=mesh, in_specs=in_specs, out_specs=out_specs, check_vma=False
    )
```

```python
import functools

import jax
import jax.numpy as jnp
from jax import lax
from jax.experimental import pallas as pl
from jax.experimental.pallas import tpu as pltpu
from jax.sharding import PartitionSpec as P

MESH = pl.DeviceIdType.MESH
F32, BF16 = jnp.float32, jnp.bfloat16
K, S, C, T = 8, 12, 12, 16
HALF = C // 2
VROWS, SROWS = K * 2 * T, S * 2 * T
OUT = 3
ROWS = 32 * OUT
Y_ORDER = (1, 0, 2, 3, 7, 6, 5, 4)


def iota(shape, dim):
    return lax.broadcasted_iota(jnp.int32, shape, dim)


def places():
    m, t, g = lax.axis_index("mode"), lax.axis_index("tm"), lax.axis_index("gz")
    near = m + 1 - 2 * lax.rem(m, 2)
    far = 3 - m
    return m, t, g, near, far


def plane_peers():
    m, t, _, _, _ = places()
    z = t // 2
    return [((m, 2 * z + core, gz), 0, True) for gz in Y_ORDER for core in range(2)]


def line_peers():
    m, t, g, near, far = places()
    core = lax.rem(t, 2)
    return [
        ((mode, 2 * z + core, g), group, group == 0)
        for z in range(8)
        for mode, group in ((far, 2), (near, 1), (m, 0))
    ]


def for_each(peers, act):
    _, t, g, _, _ = places()
    for place, group, can_be_self in peers:
        if can_be_self:
            pl.when(jnp.logical_or(place[1] != t, place[2] != g))(functools.partial(act, place, group))
        else:
            act(place, group)


def split3(x):
    high = x.astype(BF16)
    rest = x - high.astype(F32)
    mid = rest.astype(BF16)
    low = (rest - mid.astype(F32)).astype(BF16)
    return jnp.concatenate([high, mid, low], axis=0)


def same_tile():
    return (iota((32, VROWS), 0) // 2 == (iota((32, VROWS), 1) // 2) % T).astype(F32)


def partial_coefs(v, b):
    left = jnp.concatenate([b[:, c].reshape(SROWS, 128) for c in range(C)], axis=1)
    right = jnp.concatenate([v[:, c].reshape(VROWS, 128) for c in range(C)], axis=1)
    gram = lax.dot_general(left, right, (((1,), (1,)), ((), ())), preferred_element_type=F32)
    gram = gram.reshape(S, 32, VROWS) * same_tile()[None]
    x = gram.reshape(S, 4, 8, VROWS).sum(axis=1)
    x = x + pltpu.roll(x, 4, 1)
    x = x + pltpu.roll(x, 2, 1)
    sub = iota((8, VROWS), 0) // 2
    blocks = []
    for q in range(3):
        y = jnp.zeros((8, VROWS), F32)
        for i in range(4):
            y = jnp.where(sub == i, x[4 * q + i], y)
        blocks.append(y)
    y = split3(jnp.concatenate(blocks, axis=1))
    row, lane = iota((3 * VROWS, 128), 0), iota((3 * VROWS, 128), 1)
    pick = (lane == (row // VROWS) * 16 + ((row // 32) % K) * 2 + row % 2).astype(BF16)
    z = jnp.dot(y, pick, preferred_element_type=F32)
    return z[0:8] + z[8:16] + z[16:24]


def coefs_of(sums, e_ref, modes):
    sub, lane = iota((8, 128), 0), iota((8, 128), 1)
    rows = []
    for total, mode in zip(sums, modes):
        other = jnp.where(sub % 2 == 1, pltpu.roll(total, 1, 0), pltpu.roll(total, 7, 0))
        other = jnp.where(lane % 2 == 1, pltpu.roll(other, 1, 1), pltpu.roll(other, 127, 1))
        coef = total + jnp.where(sub % 2 == lane % 2, other, -other)
        eig = jnp.ones((8, 128), F32)
        for k in range(K):
            eig = jnp.where((lane // 2) % K == k, e_ref[mode * K + k], eig)
        rows.append((coef / eig).astype(BF16))
    small = jnp.concatenate(rows, axis=0)
    row, col = iota((128, 3 * VROWS), 0), iota((128, 3 * VROWS), 1)
    spread = (row == (col // VROWS) * 16 + ((col // 32) % K) * 2 + col % 2).astype(BF16)
    wide = jnp.dot(small, spread, preferred_element_type=F32)
    return jnp.concatenate(
        [
            jnp.concatenate([wide[8 * g : 8 * g + 8, q * VROWS : (q + 1) * VROWS] for q in range(3)], axis=0)
            for g in range(3)
        ],
        axis=1,
    ).astype(BF16)


def weights(wide, targets):
    n = len(targets)
    shape = (n * ROWS, 24)
    row, col = iota(shape, 0), iota(shape, 1)
    target = targets[0]
    for i in range(1, n):
        target = jnp.where(row < i * ROWS, target, targets[i])
    source = target * OUT + (row // 32) % OUT
    choose = (col == source * 2 + row % 2).astype(BF16)
    full = jnp.dot(choose, wide, preferred_element_type=F32)
    tile = jnp.concatenate([same_tile()] * (wide.shape[1] // VROWS), axis=1)
    return (full.reshape(n * OUT, 32, wide.shape[1]) * tile[None]).reshape(n * ROWS, wide.shape[1]).astype(BF16)


def kernel(
    v_hbm, b_hbm, e_hbm, o_ref,
    v, b, e, pair, first, slots1, second, slots2, send, recv,
    load_sem, pair_send, pair_recv, send1, recv1, send2, recv2, send3, recv3,
):
    m, t, g, near, far = places()
    core, z = lax.rem(t, 2), t // 2
    loads = [
        pltpu.make_async_copy(src, dst, load_sem.at[i])
        for i, (src, dst) in enumerate(((v_hbm, v), (b_hbm, b), (e_hbm, e)))
    ]
    for copy in loads:
        copy.start()

    plane, line = plane_peers(), line_peers()
    barrier = pltpu.get_barrier_semaphore()

    def greet(place, group):
        pl.semaphore_signal(barrier, inc=1, device_id=place, device_id_type=MESH)

    for_each(plane + line, greet)
    pl.semaphore_wait(barrier, len(plane) + len(line) - 2)

    loads[0].wait()
    beside = ((near, t, g), (far, t, g))
    exchange = []
    for h in range(2):
        copy = pltpu.make_async_remote_copy(
            v.at[:, pl.ds(h * HALF, HALF)], pair.at[h], pair_send.at[h], pair_recv.at[h],
            device_id=beside[h], device_id_type=MESH,
        )
        copy.start()
        exchange.append(copy)
    loads[1].wait()

    mine = partial_coefs(v, b)
    first[...] = mine
    own = g * 2 + core

    def post1(place, group):
        pltpu.make_async_remote_copy(
            first, slots1.at[own], send1, recv1, device_id=place, device_id_type=MESH
        ).start()

    for_each(plane, post1)
    slots1[own] = mine
    got = slots1.at[pl.ds(0, len(plane) - 1)]
    pltpu.make_async_copy(got, got, recv1).wait()
    total = slots1[...].sum(axis=0)

    second[...] = total

    def post2(place, group):
        pltpu.make_async_remote_copy(
            second, slots2.at[group * 8 + z], send2, recv2, device_id=place, device_id_type=MESH
        ).start()

    for_each(line, post2)
    slots2[z] = total
    got2 = slots2.at[pl.ds(0, len(line) - 1)]
    loads[2].wait()
    pltpu.make_async_copy(got2, got2, recv2).wait()
    sums = [slots2[8 * i : 8 * i + 8].sum(axis=0) for i in range(3)]

    wide = coefs_of(sums, e, (m, near, far))
    away = weights(wide, (far, near))

    def half(h, left):
        right = jnp.concatenate(
            [
                jnp.concatenate([ref[:, c0 + c].reshape(VROWS, 128) for c in range(HALF)], axis=1)
                for ref, c0 in ((v, h * HALF), (pair.at[h], 0))
            ],
            axis=0,
        )
        return jnp.dot(left, right, preferred_element_type=F32)

    def columns(w, h):
        mate = 1 + h
        return jnp.concatenate([w[:, :VROWS], w[:, mate * VROWS : (mate + 1) * VROWS]], axis=1)

    sends = []
    for h in range(2):
        exchange[h].wait_recv()
        out = half(h, columns(away[h * ROWS : (h + 1) * ROWS], h))
        for c in range(HALF):
            send[h, :, c] = out[:, c * 128 : c * 128 + 128].astype(BF16).reshape(OUT, 32, 128)
        copy = pltpu.make_async_remote_copy(
            send.at[h], recv.at[h], send3.at[h], recv3.at[h],
            device_id=beside[1 - h], device_id_type=MESH,
        )
        copy.start()
        sends.append(copy)
    home = weights(wide, (m,))
    for h in range(2):
        out = half(h, columns(home, h))
        for c in range(HALF):
            o_ref[:, h * HALF + c] = out[:, c * 128 : c * 128 + 128].reshape(OUT, 32, 128)

    for h in range(2):
        exchange[h].wait_send()
    pltpu.make_async_copy(got, got, send1).wait()
    pltpu.make_async_copy(got2, got2, send2).wait()
    for h in range(2):
        sends[h].wait_recv()
        o_ref[:, h * HALF : (h + 1) * HALF] += recv[h].astype(F32)
    for h in range(2):
        sends[h].wait_send()


def on_device(vectors, sources, eigenvalues):
    def tiles(x):
        n = x.shape[0]
        return x.reshape(n, 2, C, T, 128).transpose(0, 2, 3, 1, 4).reshape(n, C, 2 * T, 128)

    dma = pltpu.SemaphoreType.DMA
    out = pl.pallas_call(
        kernel,
        out_shape=pltpu.VMEM((OUT, C, 2 * T, 128), F32),
        in_specs=[
            pl.BlockSpec(memory_space=pltpu.HBM),
            pl.BlockSpec(memory_space=pltpu.HBM),
            pl.BlockSpec(memory_space=pltpu.HBM),
        ],
        out_specs=pl.BlockSpec(memory_space=pltpu.VMEM),
        scratch_shapes=[
            pltpu.VMEM((K, C, 2 * T, 128), BF16),
            pltpu.VMEM((S, C, 2 * T, 128), BF16),
            pltpu.SMEM((32,), F32),
            pltpu.VMEM((2, K, HALF, 2 * T, 128), BF16),
            pltpu.VMEM((8, 128), F32),
            pltpu.VMEM((16, 8, 128), F32),
            pltpu.VMEM((8, 128), F32),
            pltpu.VMEM((24, 8, 128), F32),
            pltpu.VMEM((2, OUT, HALF, 2 * T, 128), BF16),
            pltpu.VMEM((2, OUT, HALF, 2 * T, 128), BF16),
            dma((3,)), dma((2,)), dma((2,)), dma, dma, dma, dma, dma((2,)), dma((2,)),
        ],
        compiler_params=pltpu.CompilerParams(
            collective_id=0, has_side_effects=True, vmem_limit_bytes=60 * 2**20
        ),
        name="deflate",
    )(tiles(vectors), tiles(sources), eigenvalues)
    return out.reshape(OUT, C, T, 2, 128).transpose(0, 3, 1, 2, 4).reshape(OUT, 2, C, T * 128)


def solution(mesh):
    in_specs = (P("mode", None, None, ("tm", "gz")), P(None, None, None, ("tm", "gz")), P())
    out_specs = P("mode", None, None, ("tm", "gz"))
    return jax.shard_map(
        on_device, mesh=mesh, in_specs=in_specs, out_specs=out_specs, check_vma=False
    )
```

```python
import functools

import jax
import jax.numpy as jnp
from jax import lax
from jax.experimental import pallas as pl
from jax.experimental.pallas import tpu as pltpu
from jax.sharding import PartitionSpec as P

MESH = pl.DeviceIdType.MESH
F32, BF16 = jnp.float32, jnp.bfloat16
K, S, C, T = 8, 12, 12, 16
HALF = C // 2
WIDTH = 2
VROWS, SROWS = K * 2 * T, S * 2 * T
OUT = 3
ROWS = 32 * OUT
Y_ORDER = (0, 1, 2, 3, 7, 6, 5, 4)


def iota(shape, dim):
    return lax.broadcasted_iota(jnp.int32, shape, dim)


def places():
    m, t, g = lax.axis_index("mode"), lax.axis_index("tm"), lax.axis_index("gz")
    near = m + 1 - 2 * lax.rem(m, 2)
    far = 3 - m
    return m, t, g, near, far


def plane_peers():
    m, t, g, _, _ = places()
    other = t + 1 - 2 * lax.rem(t, 2)
    at = 0
    for i, y in enumerate(Y_ORDER):
        at = jnp.where(g == y, i, at)
    peers = []
    for i in range(8):
        peers.append((m, other, Y_ORDER[i]))
        if i < 7:
            peers.append((m, t, jnp.where(i < at, Y_ORDER[i], Y_ORDER[i + 1])))
    return peers


def line_peers():
    m, t, g, near, far = places()
    z, core = t // 2, lax.rem(t, 2)
    peers = []
    for i in range(8):
        peers.append(((far, 2 * i + core, g), 2))
        peers.append(((near, 2 * i + core, g), 1))
        if i < 7:
            peers.append(((m, 2 * jnp.where(i < z, i, i + 1) + core, g), 0))
    return peers


def split3(x):
    high = x.astype(BF16)
    rest = x - high.astype(F32)
    mid = rest.astype(BF16)
    low = (rest - mid.astype(F32)).astype(BF16)
    return jnp.concatenate([high, mid, low], axis=0)


def same_tile():
    return (iota((32, VROWS), 0) // 2 == (iota((32, VROWS), 1) // 2) % T).astype(F32)


def partial_coefs(v, b, tile, pick):
    left = jnp.concatenate([b[:, c].reshape(SROWS, 128) for c in range(C)], axis=1)
    right = jnp.concatenate([v[:, c].reshape(VROWS, 128) for c in range(C)], axis=1)
    gram = lax.dot_general(left, right, (((1,), (1,)), ((), ())), preferred_element_type=F32)
    gram = gram.reshape(S, 32, VROWS) * tile[...][None]
    x = gram.reshape(S, 4, 8, VROWS).sum(axis=1)
    x = x + pltpu.roll(x, 4, 1)
    x = x + pltpu.roll(x, 2, 1)
    sub = iota((8, VROWS), 0) // 2
    blocks = []
    for q in range(3):
        y = jnp.zeros((8, VROWS), F32)
        for i in range(4):
            y = jnp.where(sub == i, x[4 * q + i], y)
        blocks.append(y)
    y = split3(jnp.concatenate(blocks, axis=1))
    z = jnp.dot(y, pick[...], preferred_element_type=F32)
    return z[0:8] + z[8:16] + z[16:24]


def tables1(tile, pick):
    tile[...] = same_tile()
    row, lane = iota((3 * VROWS, 128), 0), iota((3 * VROWS, 128), 1)
    pick[...] = (lane == (row // VROWS) * 16 + ((row // 32) % K) * 2 + row % 2).astype(BF16)


def tables2(spread, choose, targets):
    row, col = iota((128, 3 * VROWS), 0), iota((128, 3 * VROWS), 1)
    spread[...] = (row == (col // VROWS) * 16 + ((col // 32) % K) * 2 + col % 2).astype(BF16)
    row, col = iota((ROWS, 24), 0), iota((ROWS, 24), 1)
    for i, target in enumerate(targets):
        choose[i] = (col == (target * OUT + row // 32) * 2 + row % 2).astype(BF16)


def coefs_of(sums, eig, spread):
    sub, lane = iota((8, 128), 0), iota((8, 128), 1)
    rows = []
    for i, total in enumerate(sums):
        other = jnp.where(sub % 2 == 1, pltpu.roll(total, 1, 0), pltpu.roll(total, 7, 0))
        other = jnp.where(lane % 2 == 1, pltpu.roll(other, 1, 1), pltpu.roll(other, 127, 1))
        coef = total + jnp.where(sub % 2 == lane % 2, other, -other)
        rows.append((coef / eig[i]).astype(BF16))
    small = jnp.concatenate(rows, axis=0)
    wide = jnp.dot(small, spread[...], preferred_element_type=F32)
    return jnp.concatenate(
        [
            jnp.concatenate([wide[8 * g : 8 * g + 8, q * VROWS : (q + 1) * VROWS] for q in range(3)], axis=0)
            for g in range(3)
        ],
        axis=1,
    ).astype(BF16)


def weights(wide, choose, tile):
    n, blocks = choose.shape[0] // ROWS, wide.shape[1] // VROWS
    full = jnp.dot(choose, wide, preferred_element_type=F32)
    same = jnp.concatenate([tile[...]] * blocks, axis=1)
    return (full.reshape(n * OUT, 32, wide.shape[1]) * same[None]).reshape(choose.shape[0], wide.shape[1]).astype(BF16)


def kernel(
    v_hbm, b_hbm, e_hbm, o_ref,
    v, b, e, tile, pick, spread, choose, eig, pair, first, slots1, second, slots2, send, recv,
    load_sem, pair_send, pair_recv, send1, recv1, send2, recv2, send3, recv3,
):
    m, t, g, near, far = places()
    core, z = lax.rem(t, 2), t // 2
    loads = [
        pltpu.make_async_copy(src, dst, load_sem.at[i])
        for i, (src, dst) in enumerate(((v_hbm, v), (b_hbm, b), (e_hbm, e)))
    ]
    for copy in loads:
        copy.start()

    plane, line = plane_peers(), line_peers()
    barrier = pltpu.get_barrier_semaphore()
    for place in plane[::-1] + [p for p, _ in line]:
        pl.semaphore_signal(barrier, inc=1, device_id=place, device_id_type=MESH)
    tables1(tile, pick)
    loads[0].wait()
    loads[1].wait()
    mine = partial_coefs(v, b, tile, pick)
    first[...] = mine
    pl.semaphore_wait(barrier, len(plane) + len(line))

    own = g * 2 + core
    for place in plane:
        pltpu.make_async_remote_copy(
            first, slots1.at[own], send1, recv1, device_id=place, device_id_type=MESH
        ).start()
    beside = ((near, t, g), (far, t, g))
    exchange = []
    for h in range(2):
        copy = pltpu.make_async_remote_copy(
            v.at[:, pl.ds(h * HALF, HALF)], pair.at[h], pair_send.at[h], pair_recv.at[h],
            device_id=beside[h], device_id_type=MESH,
        )
        copy.start()
        exchange.append(copy)
    slots1[own] = mine
    tables2(spread, choose, (far, near, m))
    loads[2].wait()
    lane = iota((8, 128), 1)
    for i, mode in enumerate((m, near, far)):
        scale = jnp.ones((8, 128), F32)
        for k in range(K):
            scale = jnp.where((lane // 2) % K == k, e[mode * K + k], scale)
        eig[i] = scale
    got = slots1.at[pl.ds(0, len(plane))]
    pltpu.make_async_copy(got, got, recv1).wait()
    total = slots1[...].sum(axis=0)

    second[...] = total
    for place, group in line:
        pltpu.make_async_remote_copy(
            second, slots2.at[group * 8 + z], send2, recv2, device_id=place, device_id_type=MESH
        ).start()
    slots2[z] = total
    got2 = slots2.at[pl.ds(0, len(line))]
    pltpu.make_async_copy(got2, got2, recv2).wait()
    sums = [slots2[8 * i : 8 * i + 8].sum(axis=0) for i in range(3)]

    wide = coefs_of(sums, eig, spread)
    away = weights(wide, choose[0:2].reshape(2 * ROWS, 24), tile)

    def rows_of(left, start, h):
        right = jnp.concatenate(
            [
                jnp.concatenate([ref[:, c0 + c].reshape(VROWS, 128) for c in range(WIDTH)], axis=1)
                for ref, c0 in ((v, start), (pair.at[h], start - h * HALF))
            ],
            axis=0,
        )
        return jnp.dot(left, right, preferred_element_type=F32)

    def columns(w, h):
        mate = 1 + h
        return jnp.concatenate([w[:, :VROWS], w[:, mate * VROWS : (mate + 1) * VROWS]], axis=1)

    left = [columns(away[h * ROWS : (h + 1) * ROWS], h) for h in range(2)]
    sends = [None] * (C // WIDTH)
    for i in range(HALF // WIDTH):
        for h in range(2):
            if i == 0:
                exchange[h].wait_recv()
            start = h * HALF + i * WIDTH
            out = rows_of(left[h], start, h)
            for c in range(WIDTH):
                send[:, start + c] = out[:, c * 128 : c * 128 + 128].astype(BF16).reshape(OUT, 32, 128)
            part = pl.ds(start, WIDTH)
            n = start // WIDTH
            sends[n] = pltpu.make_async_remote_copy(
                send.at[:, part], recv.at[:, part], send3.at[n], recv3.at[n],
                device_id=beside[1 - h], device_id_type=MESH,
            )
            sends[n].start()
    home = weights(wide, choose[2], tile)
    for h in range(2):
        left = columns(home, h)
        for start in range(h * HALF, (h + 1) * HALF, WIDTH):
            out = rows_of(left, start, h)
            for c in range(WIDTH):
                o_ref[:, start + c] = out[:, c * 128 : c * 128 + 128].reshape(OUT, 32, 128)

    for h in range(2):
        exchange[h].wait_send()
    pltpu.make_async_copy(got, got, send1).wait()
    pltpu.make_async_copy(got2, got2, send2).wait()
    for i, copy in enumerate(sends):
        copy.wait_recv()
        part = slice(i * WIDTH, (i + 1) * WIDTH)
        o_ref[:, part] += recv[:, part].astype(F32)
    for copy in sends:
        copy.wait_send()


def on_device(vectors, sources, eigenvalues):
    def tiles(x):
        n = x.shape[0]
        return x.reshape(n, 2, C, T, 128).transpose(0, 2, 3, 1, 4).reshape(n, C, 2 * T, 128)

    dma = pltpu.SemaphoreType.DMA
    out = pl.pallas_call(
        kernel,
        out_shape=pltpu.VMEM((OUT, C, 2 * T, 128), F32),
        in_specs=[
            pl.BlockSpec(memory_space=pltpu.HBM),
            pl.BlockSpec(memory_space=pltpu.HBM),
            pl.BlockSpec(memory_space=pltpu.HBM),
        ],
        out_specs=pl.BlockSpec(memory_space=pltpu.VMEM),
        scratch_shapes=[
            pltpu.VMEM((K, C, 2 * T, 128), BF16),
            pltpu.VMEM((S, C, 2 * T, 128), BF16),
            pltpu.SMEM((32,), F32),
            pltpu.VMEM((32, VROWS), F32),
            pltpu.VMEM((3 * VROWS, 128), BF16),
            pltpu.VMEM((128, 3 * VROWS), BF16),
            pltpu.VMEM((3, ROWS, 24), BF16),
            pltpu.VMEM((3, 8, 128), F32),
            pltpu.VMEM((2, K, HALF, 2 * T, 128), BF16),
            pltpu.VMEM((8, 128), F32),
            pltpu.VMEM((16, 8, 128), F32),
            pltpu.VMEM((8, 128), F32),
            pltpu.VMEM((24, 8, 128), F32),
            pltpu.VMEM((OUT, C, 2 * T, 128), BF16),
            pltpu.VMEM((OUT, C, 2 * T, 128), BF16),
            dma((3,)), dma((2,)), dma((2,)), dma, dma, dma, dma, dma((C // WIDTH,)), dma((C // WIDTH,)),
        ],
        compiler_params=pltpu.CompilerParams(
            collective_id=0, has_side_effects=True, vmem_limit_bytes=60 * 2**20
        ),
        name="deflate",
    )(tiles(vectors), tiles(sources), eigenvalues)
    return out.reshape(OUT, C, T, 2, 128).transpose(0, 3, 1, 2, 4).reshape(OUT, 2, C, T * 128)


def solution(mesh):
    in_specs = (P("mode", None, None, ("tm", "gz")), P(None, None, None, ("tm", "gz")), P())
    out_specs = P("mode", None, None, ("tm", "gz"))
    return jax.shard_map(
        on_device, mesh=mesh, in_specs=in_specs, out_specs=out_specs, check_vma=False
    )
```

```python
import functools

import jax
import jax.numpy as jnp
from jax import lax
from jax.experimental import pallas as pl
from jax.experimental.pallas import tpu as pltpu
from jax.sharding import PartitionSpec as P

MESH = pl.DeviceIdType.MESH
F32, BF16 = jnp.float32, jnp.bfloat16
K, S, C, T = 8, 12, 12, 16
HALF = C // 2
WIDTH = 3
VROWS, SROWS = K * 2 * T, S * 2 * T
OUT = 3
ROWS = 32 * OUT
Y_ORDER = (0, 1, 2, 3, 7, 6, 5, 4)


def iota(shape, dim):
    return lax.broadcasted_iota(jnp.int32, shape, dim)


def places():
    m, t, g = lax.axis_index("mode"), lax.axis_index("tm"), lax.axis_index("gz")
    near = m + 1 - 2 * lax.rem(m, 2)
    far = 3 - m
    return m, t, g, near, far


def plane_peers():
    m, t, g, _, _ = places()
    other = t + 1 - 2 * lax.rem(t, 2)
    at = 0
    for i, y in enumerate(Y_ORDER):
        at = jnp.where(g == y, i, at)
    peers = []
    for i in range(8):
        peers.append((m, other, Y_ORDER[i]))
        if i < 7:
            peers.append((m, t, jnp.where(i < at, Y_ORDER[i], Y_ORDER[i + 1])))
    return peers


def line_peers():
    m, t, g, near, far = places()
    z, core = t // 2, lax.rem(t, 2)
    peers = []
    for i in range(8):
        peers.append(((far, 2 * i + core, g), 2))
        peers.append(((near, 2 * i + core, g), 1))
        if i < 7:
            peers.append(((m, 2 * jnp.where(i < z, i, i + 1) + core, g), 0))
    return peers


def split3(x):
    high = x.astype(BF16)
    rest = x - high.astype(F32)
    mid = rest.astype(BF16)
    low = (rest - mid.astype(F32)).astype(BF16)
    return jnp.concatenate([high, mid, low], axis=0)


def same_tile():
    return (iota((32, VROWS), 0) // 2 == (iota((32, VROWS), 1) // 2) % T).astype(F32)


def partial_coefs(v, b, tile, pick):
    left = jnp.concatenate([b[:, c].reshape(SROWS, 128) for c in range(C)], axis=1)
    right = jnp.concatenate([v[:, c].reshape(VROWS, 128) for c in range(C)], axis=1)
    gram = lax.dot_general(left, right, (((1,), (1,)), ((), ())), preferred_element_type=F32)
    gram = gram.reshape(S, 32, VROWS) * tile[...][None]
    x = gram.reshape(S, 4, 8, VROWS).sum(axis=1)
    x = x + pltpu.roll(x, 4, 1)
    x = x + pltpu.roll(x, 2, 1)
    sub = iota((8, VROWS), 0) // 2
    blocks = []
    for q in range(3):
        y = jnp.zeros((8, VROWS), F32)
        for i in range(4):
            y = jnp.where(sub == i, x[4 * q + i], y)
        blocks.append(y)
    y = split3(jnp.concatenate(blocks, axis=1))
    z = jnp.dot(y, pick[...], preferred_element_type=F32)
    return z[0:8] + z[8:16] + z[16:24]


def tables1(tile, pick):
    tile[...] = same_tile()
    row, lane = iota((3 * VROWS, 128), 0), iota((3 * VROWS, 128), 1)
    pick[...] = (lane == (row // VROWS) * 16 + ((row // 32) % K) * 2 + row % 2).astype(BF16)


def tables2(spread, row_of, targets):
    row, col = iota((128, VROWS), 0), iota((128, VROWS), 1)
    spread[...] = jnp.logical_and(row < 48, row % 16 == (col // 32) * 2 + col % 2).astype(BF16)
    sub, lane = iota((8, 128), 0), iota((8, 128), 1)
    for i, target in enumerate(targets):
        for j in range(OUT):
            source = target * OUT + j
            here = jnp.logical_and(sub // 2 == source % 4, lane // 16 == source // 4)
            row_of[i * OUT + j] = here.astype(F32)


def coefs_of(sums, inverse):
    sub, lane = iota((8, 128), 0), iota((8, 128), 1)
    blocks = []
    for i, total in enumerate(sums):
        other = jnp.where(sub % 2 == 1, pltpu.roll(total, 1, 0), pltpu.roll(total, 7, 0))
        other = jnp.where(lane % 2 == 1, pltpu.roll(other, 1, 1), pltpu.roll(other, 127, 1))
        coef = total + jnp.where(sub % 2 == lane % 2, other, -other)
        blocks.append((coef * inverse[i]).astype(BF16).astype(F32))
    return blocks


def weights(blocks, row_of, wanted, spread, tile):
    small = []
    for target, use in wanted:
        for j in range(OUT):
            for g in use:
                x = blocks[g] * row_of[target * OUT + j]
                x = x + pltpu.roll(x, 4, 0)
                small.append(x + pltpu.roll(x, 2, 0))
    wide = jnp.dot(jnp.concatenate(small, axis=0).astype(BF16), spread[...], preferred_element_type=F32)
    result, at = [], 0
    same = tile[...]
    for target, use in wanted:
        rows = []
        for j in range(OUT):
            row = []
            for g in use:
                row.append(jnp.concatenate([wide[at : at + 8]] * 4, axis=0) * same)
                at += 8
            rows.append(jnp.concatenate(row, axis=1))
        result.append(jnp.concatenate(rows, axis=0).astype(BF16))
    return result


def kernel(
    v_hbm, b_hbm, e_hbm, o_ref,
    v, b, e, tile, pick, spread, row_of, inverse, pair, first, slots1, second, slots2, send, recv,
    load_sem, pair_send, pair_recv, send1, recv1, send2, recv2, send3, recv3,
):
    m, t, g, near, far = places()
    core, z = lax.rem(t, 2), t // 2
    loads = [
        pltpu.make_async_copy(src, dst, load_sem.at[i])
        for i, (src, dst) in enumerate(((v_hbm, v), (b_hbm, b), (e_hbm, e)))
    ]
    for copy in loads:
        copy.start()

    plane, line = plane_peers(), line_peers()
    barrier = pltpu.get_barrier_semaphore()
    for place in plane[::-1] + [p for p, _ in line]:
        pl.semaphore_signal(barrier, inc=1, device_id=place, device_id_type=MESH)
    tables1(tile, pick)
    loads[0].wait()
    loads[1].wait()
    mine = partial_coefs(v, b, tile, pick)
    first[...] = mine
    pl.semaphore_wait(barrier, len(plane) + len(line))

    own = g * 2 + core
    for place in plane:
        pltpu.make_async_remote_copy(
            first, slots1.at[own], send1, recv1, device_id=place, device_id_type=MESH
        ).start()
    beside = ((near, t, g), (far, t, g))
    exchange = []
    for h in range(2):
        copy = pltpu.make_async_remote_copy(
            v.at[:, pl.ds(h * HALF, HALF)], pair.at[h], pair_send.at[h], pair_recv.at[h],
            device_id=beside[h], device_id_type=MESH,
        )
        copy.start()
        exchange.append(copy)
    slots1[own] = mine
    tables2(spread, row_of, (far, near, m))
    loads[2].wait()
    lane = iota((8, 128), 1)
    for i, mode in enumerate((m, near, far)):
        scale = jnp.ones((8, 128), F32)
        for k in range(K):
            scale = jnp.where((lane // 2) % K == k, e[mode * K + k], scale)
        inverse[i] = 1.0 / scale
    got = slots1.at[pl.ds(0, len(plane))]
    pltpu.make_async_copy(got, got, recv1).wait()
    total = slots1[...].sum(axis=0)

    second[...] = total
    for place, group in line:
        pltpu.make_async_remote_copy(
            second, slots2.at[group * 8 + z], send2, recv2, device_id=place, device_id_type=MESH
        ).start()
    slots2[z] = total
    got2 = slots2.at[pl.ds(0, len(line))]
    pltpu.make_async_copy(got2, got2, recv2).wait()
    sums = [slots2[8 * i : 8 * i + 8].sum(axis=0) for i in range(3)]

    blocks = coefs_of(sums, inverse)
    left = weights(blocks, row_of, ((0, (0, 1)), (1, (0, 2))), spread, tile)

    def rows_of(left, start, h):
        right = jnp.concatenate(
            [
                jnp.concatenate([ref[:, c0 + c].reshape(VROWS, 128) for c in range(WIDTH)], axis=1)
                for ref, c0 in ((v, start), (pair.at[h], start - h * HALF))
            ],
            axis=0,
        )
        return jnp.dot(left, right, preferred_element_type=F32)

    sends = [None] * (C // WIDTH)
    for i in range(HALF // WIDTH):
        for h in range(2):
            if i == 0:
                exchange[h].wait_recv()
            start = h * HALF + i * WIDTH
            out = rows_of(left[h], start, h)
            for c in range(WIDTH):
                send[:, start + c] = out[:, c * 128 : c * 128 + 128].astype(BF16).reshape(OUT, 32, 128)
            part = pl.ds(start, WIDTH)
            n = start // WIDTH
            sends[n] = pltpu.make_async_remote_copy(
                send.at[:, part], recv.at[:, part], send3.at[n], recv3.at[n],
                device_id=beside[1 - h], device_id_type=MESH,
            )
            sends[n].start()
    home = weights(blocks, row_of, ((2, (0, 1)), (2, (0, 2))), spread, tile)
    for h in range(2):
        for start in range(h * HALF, (h + 1) * HALF, WIDTH):
            out = rows_of(home[h], start, h)
            for c in range(WIDTH):
                o_ref[:, start + c] = out[:, c * 128 : c * 128 + 128].reshape(OUT, 32, 128)

    for h in range(2):
        exchange[h].wait_send()
    pltpu.make_async_copy(got, got, send1).wait()
    pltpu.make_async_copy(got2, got2, send2).wait()
    for i, copy in enumerate(sends):
        copy.wait_recv()
        part = slice(i * WIDTH, (i + 1) * WIDTH)
        o_ref[:, part] += recv[:, part].astype(F32)
    for copy in sends:
        copy.wait_send()


def on_device(vectors, sources, eigenvalues):
    def tiles(x):
        n = x.shape[0]
        return x.reshape(n, 2, C, T, 128).transpose(0, 2, 3, 1, 4).reshape(n, C, 2 * T, 128)

    dma = pltpu.SemaphoreType.DMA
    out = pl.pallas_call(
        kernel,
        out_shape=pltpu.VMEM((OUT, C, 2 * T, 128), F32),
        in_specs=[
            pl.BlockSpec(memory_space=pltpu.HBM),
            pl.BlockSpec(memory_space=pltpu.HBM),
            pl.BlockSpec(memory_space=pltpu.HBM),
        ],
        out_specs=pl.BlockSpec(memory_space=pltpu.VMEM),
        scratch_shapes=[
            pltpu.VMEM((K, C, 2 * T, 128), BF16),
            pltpu.VMEM((S, C, 2 * T, 128), BF16),
            pltpu.SMEM((32,), F32),
            pltpu.VMEM((32, VROWS), F32),
            pltpu.VMEM((3 * VROWS, 128), BF16),
            pltpu.VMEM((128, VROWS), BF16),
            pltpu.VMEM((3 * OUT, 8, 128), F32),
            pltpu.VMEM((3, 8, 128), F32),
            pltpu.VMEM((2, K, HALF, 2 * T, 128), BF16),
            pltpu.VMEM((8, 128), F32),
            pltpu.VMEM((16, 8, 128), F32),
            pltpu.VMEM((8, 128), F32),
            pltpu.VMEM((24, 8, 128), F32),
            pltpu.VMEM((OUT, C, 2 * T, 128), BF16),
            pltpu.VMEM((OUT, C, 2 * T, 128), BF16),
            dma((3,)), dma((2,)), dma((2,)), dma, dma, dma, dma, dma((C // WIDTH,)), dma((C // WIDTH,)),
        ],
        compiler_params=pltpu.CompilerParams(
            collective_id=0, has_side_effects=True, vmem_limit_bytes=60 * 2**20
        ),
        name="deflate",
    )(tiles(vectors), tiles(sources), eigenvalues)
    return out.reshape(OUT, C, T, 2, 128).transpose(0, 3, 1, 2, 4).reshape(OUT, 2, C, T * 128)


def solution(mesh):
    in_specs = (P("mode", None, None, ("tm", "gz")), P(None, None, None, ("tm", "gz")), P())
    out_specs = P("mode", None, None, ("tm", "gz"))
    return jax.shard_map(
        on_device, mesh=mesh, in_specs=in_specs, out_specs=out_specs, check_vma=False
    )
```

```python
import functools

import jax
import jax.numpy as jnp
from jax import lax
from jax.experimental import pallas as pl
from jax.experimental.pallas import tpu as pltpu
from jax.sharding import PartitionSpec as P

MESH = pl.DeviceIdType.MESH
F32, BF16 = jnp.float32, jnp.bfloat16
K, S, C, T = 8, 12, 12, 16
HALF = C // 2
WIDTH = 3
VROWS, SROWS = K * 2 * T, S * 2 * T
OUT = 3
ROWS = 32 * OUT
Y_ORDER = (0, 1, 2, 3, 7, 6, 5, 4)


def iota(shape, dim):
    return lax.broadcasted_iota(jnp.int32, shape, dim)


def places():
    m, t, g = lax.axis_index("mode"), lax.axis_index("tm"), lax.axis_index("gz")
    near = m + 1 - 2 * lax.rem(m, 2)
    far = 3 - m
    return m, t, g, near, far


def plane_peers():
    m, t, g, _, _ = places()
    other = t + 1 - 2 * lax.rem(t, 2)
    at = 0
    for i, y in enumerate(Y_ORDER):
        at = jnp.where(g == y, i, at)
    peers = []
    for i in range(8):
        peers.append((m, other, Y_ORDER[i]))
        if i < 7:
            peers.append((m, t, jnp.where(i < at, Y_ORDER[i], Y_ORDER[i + 1])))
    return peers


def split3(x):
    high = x.astype(BF16)
    rest = x - high.astype(F32)
    mid = rest.astype(BF16)
    low = (rest - mid.astype(F32)).astype(BF16)
    return jnp.concatenate([high, mid, low], axis=0)


def same_tile():
    return (iota((32, VROWS), 0) // 2 == (iota((32, VROWS), 1) // 2) % T).astype(F32)


def partial_coefs(v, b, tile, pick):
    left = jnp.concatenate([b[:, c].reshape(SROWS, 128) for c in range(C)], axis=1)
    right = jnp.concatenate([v[:, c].reshape(VROWS, 128) for c in range(C)], axis=1)
    gram = lax.dot_general(left, right, (((1,), (1,)), ((), ())), preferred_element_type=F32)
    gram = gram.reshape(S, 32, VROWS) * tile[...][None]
    x = gram.reshape(S, 4, 8, VROWS).sum(axis=1)
    x = x + pltpu.roll(x, 4, 1)
    x = x + pltpu.roll(x, 2, 1)
    sub = iota((8, VROWS), 0) // 2
    blocks = []
    for q in range(3):
        y = jnp.zeros((8, VROWS), F32)
        for i in range(4):
            y = jnp.where(sub == i, x[4 * q + i], y)
        blocks.append(y)
    y = split3(jnp.concatenate(blocks, axis=1))
    z = jnp.dot(y, pick[...], preferred_element_type=F32)
    return z[0:8] + z[8:16] + z[16:24]


def tables1(tile, pick):
    tile[...] = same_tile()
    row, lane = iota((3 * VROWS, 128), 0), iota((3 * VROWS, 128), 1)
    pick[...] = (lane == (row // VROWS) * 16 + ((row // 32) % K) * 2 + row % 2).astype(BF16)


def tables2(spread, row_of, targets):
    row, col = iota((128, VROWS), 0), iota((128, VROWS), 1)
    spread[...] = jnp.logical_and(row < 48, row % 16 == (col // 32) * 2 + col % 2).astype(BF16)
    sub, lane = iota((8, 128), 0), iota((8, 128), 1)
    for i, target in enumerate(targets):
        for j in range(OUT):
            source = target * OUT + j
            here = jnp.logical_and(sub // 2 == source % 4, lane // 16 == source // 4)
            row_of[i * OUT + j] = here.astype(F32)


def coefs_of(sums, inverse):
    sub, lane = iota((8, 128), 0), iota((8, 128), 1)
    blocks = []
    for i, total in enumerate(sums):
        other = jnp.where(sub % 2 == 1, pltpu.roll(total, 1, 0), pltpu.roll(total, 7, 0))
        other = jnp.where(lane % 2 == 1, pltpu.roll(other, 1, 1), pltpu.roll(other, 127, 1))
        coef = total + jnp.where(sub % 2 == lane % 2, other, -other)
        blocks.append((coef * inverse[i]).astype(BF16).astype(F32))
    return blocks


def weights(blocks, row_of, wanted, spread, tile):
    small = []
    for target, use in wanted:
        for j in range(OUT):
            for g in use:
                x = blocks[g] * row_of[target * OUT + j]
                x = x + pltpu.roll(x, 4, 0)
                small.append(x + pltpu.roll(x, 2, 0))
    wide = jnp.dot(jnp.concatenate(small, axis=0).astype(BF16), spread[...], preferred_element_type=F32)
    result, at = [], 0
    same = tile[...]
    for target, use in wanted:
        rows = []
        for j in range(OUT):
            row = []
            for g in use:
                row.append(jnp.concatenate([wide[at : at + 8]] * 4, axis=0) * same)
                at += 8
            rows.append(jnp.concatenate(row, axis=1))
        result.append(jnp.concatenate(rows, axis=0).astype(BF16))
    return result


def kernel(
    v_hbm, b_hbm, e_hbm, o_ref,
    v, b, e, tile, pick, spread, row_of, inverse, pair, first, slots1, second, slots2, send, recv,
    load_sem, pair_send, pair_recv, send1, recv1, send2, recv2, send3, recv3, entered,
):
    m, t, g, near, far = places()
    core, z = lax.rem(t, 2), t // 2
    loads = [
        pltpu.make_async_copy(src, dst, load_sem.at[i])
        for i, (src, dst) in enumerate(((v_hbm, v), (b_hbm, b), (e_hbm, e)))
    ]
    for copy in loads:
        copy.start()

    plane = plane_peers()
    barrier = pltpu.get_barrier_semaphore()
    beside = ((near, t, g), (far, t, g))
    groups = ((far, 2), (near, 1), (m, 0))

    def signal(sem, place):
        pl.semaphore_signal(sem, inc=1, device_id=place, device_id_type=MESH)

    def higher(act):
        for i in range(7, 0, -1):
            pl.when(i > z)(functools.partial(act, i))

    def lower(act):
        for i in range(7):
            pl.when(i < z)(functools.partial(act, i))

    def greet(i):
        for mode, _ in groups:
            signal(barrier, (mode, 2 * i + core, g))

    def invite(i):
        for mode, _ in groups:
            signal(entered, (mode, 2 * i + core, g))

    for place in plane[::-1] + list(beside):
        signal(barrier, place)
    higher(greet)
    tables1(tile, pick)
    loads[0].wait()
    loads[1].wait()
    mine = partial_coefs(v, b, tile, pick)
    first[...] = mine
    pl.semaphore_wait(barrier, len(plane) + len(beside) + 3 * z)

    own = g * 2 + core
    for place in plane:
        pltpu.make_async_remote_copy(
            first, slots1.at[own], send1, recv1, device_id=place, device_id_type=MESH
        ).start()
    exchange = []
    for h in range(2):
        copy = pltpu.make_async_remote_copy(
            v.at[:, pl.ds(h * HALF, HALF)], pair.at[h], pair_send.at[h], pair_recv.at[h],
            device_id=beside[h], device_id_type=MESH,
        )
        copy.start()
        exchange.append(copy)
    lower(invite)
    slots1[own] = mine
    tables2(spread, row_of, (far, near, m))
    loads[2].wait()
    lane = iota((8, 128), 1)
    for i, mode in enumerate((m, near, far)):
        scale = jnp.ones((8, 128), F32)
        for k in range(K):
            scale = jnp.where((lane // 2) % K == k, e[mode * K + k], scale)
        inverse[i] = 1.0 / scale
    got = slots1.at[pl.ds(0, len(plane))]
    pltpu.make_async_copy(got, got, recv1).wait()
    total = slots1[...].sum(axis=0)

    second[...] = total

    def post(place, group):
        pltpu.make_async_remote_copy(
            second, slots2.at[group * 8 + z], send2, recv2, device_id=place, device_id_type=MESH
        ).start()

    def post_all(i):
        for mode, group in groups:
            post((mode, 2 * i + core, g), group)

    lower(post_all)
    post(beside[1], 2)
    post(beside[0], 1)
    slots2[z] = total

    @pl.when(z < 7)
    def _():
        pl.semaphore_wait(entered, 3 * (7 - z))
        higher(post_all)

    got2 = slots2.at[pl.ds(0, 23)]
    pltpu.make_async_copy(got2, got2, recv2).wait()
    sums = [slots2[8 * i : 8 * i + 8].sum(axis=0) for i in range(3)]

    blocks = coefs_of(sums, inverse)
    left = weights(blocks, row_of, ((0, (0, 1)), (1, (0, 2))), spread, tile)

    def rows_of(left, start, h):
        right = jnp.concatenate(
            [
                jnp.concatenate([ref[:, c0 + c].reshape(VROWS, 128) for c in range(WIDTH)], axis=1)
                for ref, c0 in ((v, start), (pair.at[h], start - h * HALF))
            ],
            axis=0,
        )
        return jnp.dot(left, right, preferred_element_type=F32)

    sends = [None] * (C // WIDTH)
    for i in range(HALF // WIDTH):
        for h in range(2):
            if i == 0:
                exchange[h].wait_recv()
            start = h * HALF + i * WIDTH
            out = rows_of(left[h], start, h)
            for c in range(WIDTH):
                send[:, start + c] = out[:, c * 128 : c * 128 + 128].astype(BF16).reshape(OUT, 32, 128)
            part = pl.ds(start, WIDTH)
            n = start // WIDTH
            sends[n] = pltpu.make_async_remote_copy(
                send.at[:, part], recv.at[:, part], send3.at[n], recv3.at[n],
                device_id=beside[1 - h], device_id_type=MESH,
            )
            sends[n].start()
    home = weights(blocks, row_of, ((2, (0, 1)), (2, (0, 2))), spread, tile)
    for h in range(2):
        for start in range(h * HALF, (h + 1) * HALF, WIDTH):
            out = rows_of(home[h], start, h)
            for c in range(WIDTH):
                o_ref[:, start + c] = out[:, c * 128 : c * 128 + 128].reshape(OUT, 32, 128)

    for h in range(2):
        exchange[h].wait_send()
    pltpu.make_async_copy(got, got, send1).wait()
    pltpu.make_async_copy(got2, got2, send2).wait()
    for i, copy in enumerate(sends):
        copy.wait_recv()
        part = slice(i * WIDTH, (i + 1) * WIDTH)
        o_ref[:, part] += recv[:, part].astype(F32)
    for copy in sends:
        copy.wait_send()


def on_device(vectors, sources, eigenvalues):
    def tiles(x):
        n = x.shape[0]
        return x.reshape(n, 2, C, T, 128).transpose(0, 2, 3, 1, 4).reshape(n, C, 2 * T, 128)

    dma = pltpu.SemaphoreType.DMA
    out = pl.pallas_call(
        kernel,
        out_shape=pltpu.VMEM((OUT, C, 2 * T, 128), F32),
        in_specs=[
            pl.BlockSpec(memory_space=pltpu.HBM),
            pl.BlockSpec(memory_space=pltpu.HBM),
            pl.BlockSpec(memory_space=pltpu.HBM),
        ],
        out_specs=pl.BlockSpec(memory_space=pltpu.VMEM),
        scratch_shapes=[
            pltpu.VMEM((K, C, 2 * T, 128), BF16),
            pltpu.VMEM((S, C, 2 * T, 128), BF16),
            pltpu.SMEM((32,), F32),
            pltpu.VMEM((32, VROWS), F32),
            pltpu.VMEM((3 * VROWS, 128), BF16),
            pltpu.VMEM((128, VROWS), BF16),
            pltpu.VMEM((3 * OUT, 8, 128), F32),
            pltpu.VMEM((3, 8, 128), F32),
            pltpu.VMEM((2, K, HALF, 2 * T, 128), BF16),
            pltpu.VMEM((8, 128), F32),
            pltpu.VMEM((16, 8, 128), F32),
            pltpu.VMEM((8, 128), F32),
            pltpu.VMEM((24, 8, 128), F32),
            pltpu.VMEM((OUT, C, 2 * T, 128), BF16),
            pltpu.VMEM((OUT, C, 2 * T, 128), BF16),
            dma((3,)), dma((2,)), dma((2,)), dma, dma, dma, dma, dma((C // WIDTH,)), dma((C // WIDTH,)),
            pltpu.SemaphoreType.REGULAR,
        ],
        compiler_params=pltpu.CompilerParams(
            collective_id=0, has_side_effects=True, vmem_limit_bytes=60 * 2**20
        ),
        name="deflate",
    )(tiles(vectors), tiles(sources), eigenvalues)
    return out.reshape(OUT, C, T, 2, 128).transpose(0, 3, 1, 2, 4).reshape(OUT, 2, C, T * 128)


def solution(mesh):
    in_specs = (P("mode", None, None, ("tm", "gz")), P(None, None, None, ("tm", "gz")), P())
    out_specs = P("mode", None, None, ("tm", "gz"))
    return jax.shard_map(
        on_device, mesh=mesh, in_specs=in_specs, out_specs=out_specs, check_vma=False
    )
```

```python
import functools

import jax
import jax.numpy as jnp
from jax import lax
from jax.experimental import pallas as pl
from jax.experimental.pallas import tpu as pltpu
from jax.sharding import PartitionSpec as P

MESH = pl.DeviceIdType.MESH
F32, BF16 = jnp.float32, jnp.bfloat16
K, S, C, T = 8, 12, 12, 16
HALF = C // 2
WIDTH = 3
VROWS, SROWS = K * 2 * T, S * 2 * T
OUT = 3
ROWS = 32 * OUT
Y_ORDER = (0, 1, 2, 3, 7, 6, 5, 4)


def iota(shape, dim):
    return lax.broadcasted_iota(jnp.int32, shape, dim)


def places():
    m, t, g = lax.axis_index("mode"), lax.axis_index("tm"), lax.axis_index("gz")
    near = m + 1 - 2 * lax.rem(m, 2)
    far = 3 - m
    return m, t, g, near, far


def plane_peers():
    m, t, g, _, _ = places()
    other = t + 1 - 2 * lax.rem(t, 2)
    at = 0
    for i, y in enumerate(Y_ORDER):
        at = jnp.where(g == y, i, at)
    peers = []
    for i in range(8):
        peers.append((m, other, Y_ORDER[i]))
        if i < 7:
            peers.append((m, t, jnp.where(i < at, Y_ORDER[i], Y_ORDER[i + 1])))
    return peers


def split3(x):
    high = x.astype(BF16)
    rest = x - high.astype(F32)
    mid = rest.astype(BF16)
    low = (rest - mid.astype(F32)).astype(BF16)
    return jnp.concatenate([high, mid, low], axis=0)


def same_tile():
    return (iota((32, VROWS), 0) // 2 == (iota((32, VROWS), 1) // 2) % T).astype(F32)


def partial_coefs(v, b, tile, pick):
    left = jnp.concatenate([b[:, c].reshape(SROWS, 128) for c in range(C)], axis=1)
    right = jnp.concatenate([v[:, c].reshape(VROWS, 128) for c in range(C)], axis=1)
    gram = lax.dot_general(left, right, (((1,), (1,)), ((), ())), preferred_element_type=F32)
    gram = gram.reshape(S, 32, VROWS) * tile[...][None]
    x = gram.reshape(S, 4, 8, VROWS).sum(axis=1)
    x = x + pltpu.roll(x, 4, 1)
    x = x + pltpu.roll(x, 2, 1)
    sub = iota((8, VROWS), 0) // 2
    blocks = []
    for q in range(3):
        y = jnp.zeros((8, VROWS), F32)
        for i in range(4):
            y = jnp.where(sub == i, x[4 * q + i], y)
        blocks.append(y)
    y = split3(jnp.concatenate(blocks, axis=1))
    z = jnp.dot(y, pick[...], preferred_element_type=F32)
    z = z[0:8] + z[8:16] + z[16:24]
    return jnp.where(iota((4, 128), 1) < 64, z[0:4], pltpu.roll(z[4:8], 64, 1))


def tables1(tile, pick):
    tile[...] = same_tile()
    row, lane = iota((3 * VROWS, 128), 0), iota((3 * VROWS, 128), 1)
    pick[...] = (lane == (row // VROWS) * 16 + ((row // 32) % K) * 2 + row % 2).astype(BF16)


def tables2(spread, row_of, targets):
    row, col = iota((128, VROWS), 0), iota((128, VROWS), 1)
    spread[...] = jnp.logical_and(row < 48, row % 16 == (col // 32) * 2 + col % 2).astype(BF16)
    sub, lane = iota((8, 128), 0), iota((8, 128), 1)
    for i, target in enumerate(targets):
        for j in range(OUT):
            source = target * OUT + j
            here = jnp.logical_and(sub // 2 == source % 4, lane // 16 == source // 4)
            row_of[i * OUT + j] = here.astype(F32)


def coefs_of(sums, inverse):
    sub, lane = iota((8, 128), 0), iota((8, 128), 1)
    blocks = []
    for i, total in enumerate(sums):
        other = jnp.where(sub % 2 == 1, pltpu.roll(total, 1, 0), pltpu.roll(total, 7, 0))
        other = jnp.where(lane % 2 == 1, pltpu.roll(other, 1, 1), pltpu.roll(other, 127, 1))
        coef = total + jnp.where(sub % 2 == lane % 2, other, -other)
        blocks.append((coef * inverse[i]).astype(BF16).astype(F32))
    return blocks


def weights(blocks, row_of, wanted, spread, tile):
    small = []
    for target, use in wanted:
        for j in range(OUT):
            for g in use:
                x = blocks[g] * row_of[target * OUT + j]
                x = x + pltpu.roll(x, 4, 0)
                small.append(x + pltpu.roll(x, 2, 0))
    wide = jnp.dot(jnp.concatenate(small, axis=0).astype(BF16), spread[...], preferred_element_type=F32)
    result, at = [], 0
    same = tile[...]
    for target, use in wanted:
        rows = []
        for j in range(OUT):
            row = []
            for g in use:
                row.append(jnp.concatenate([wide[at : at + 8]] * 4, axis=0) * same)
                at += 8
            rows.append(jnp.concatenate(row, axis=1))
        result.append(jnp.concatenate(rows, axis=0).astype(BF16))
    return result


def kernel(
    v_hbm, b_hbm, e_hbm, o_ref,
    v, b, e, tile, pick, spread, row_of, inverse, pair, first, slots1, second, slots2, send, recv,
    load_sem, pair_send, pair_recv, send1, recv1, send2, recv2, send3, recv3, entered,
):
    m, t, g, near, far = places()
    core, z = lax.rem(t, 2), t // 2
    loads = [
        pltpu.make_async_copy(src, dst, load_sem.at[i])
        for i, (src, dst) in enumerate(((v_hbm, v), (b_hbm, b), (e_hbm, e)))
    ]
    for copy in loads:
        copy.start()

    plane = plane_peers()
    barrier = pltpu.get_barrier_semaphore()
    beside = ((near, t, g), (far, t, g))
    groups = ((far, 2), (near, 1), (m, 0))

    def signal(sem, place):
        pl.semaphore_signal(sem, inc=1, device_id=place, device_id_type=MESH)

    def higher(act):
        for i in range(7, 0, -1):
            pl.when(i > z)(functools.partial(act, i))

    def lower(act):
        for i in range(7):
            pl.when(i < z)(functools.partial(act, i))

    def greet(i):
        for mode, _ in groups:
            signal(barrier, (mode, 2 * i + core, g))

    def invite(i):
        for mode, _ in groups:
            signal(entered, (mode, 2 * i + core, g))

    for place in plane[::-1] + list(beside):
        signal(barrier, place)
    higher(greet)
    tables1(tile, pick)
    loads[0].wait()
    loads[1].wait()
    mine = partial_coefs(v, b, tile, pick)
    first[...] = mine
    pl.semaphore_wait(barrier, len(plane) + len(beside) + 3 * z)

    own = g * 2 + core
    for place in plane:
        pltpu.make_async_remote_copy(
            first, slots1.at[own], send1, recv1, device_id=place, device_id_type=MESH
        ).start()
    exchange = []
    for h in range(2):
        copy = pltpu.make_async_remote_copy(
            v.at[:, pl.ds(h * HALF, HALF)], pair.at[h], pair_send.at[h], pair_recv.at[h],
            device_id=beside[h], device_id_type=MESH,
        )
        copy.start()
        exchange.append(copy)
    lower(invite)
    slots1[own] = mine
    tables2(spread, row_of, (far, near, m))
    loads[2].wait()
    lane = iota((8, 128), 1)
    for i, mode in enumerate((m, near, far)):
        scale = jnp.ones((8, 128), F32)
        for k in range(K):
            scale = jnp.where((lane // 2) % K == k, e[mode * K + k], scale)
        inverse[i] = 1.0 / scale
    got = slots1.at[pl.ds(0, len(plane))]
    pltpu.make_async_copy(got, got, recv1).wait()
    total = slots1[...].sum(axis=0)

    second[...] = total

    def post(place, group):
        pltpu.make_async_remote_copy(
            second, slots2.at[group * 8 + z], send2, recv2, device_id=place, device_id_type=MESH
        ).start()

    def post_all(i):
        for mode, group in groups:
            post((mode, 2 * i + core, g), group)

    lower(post_all)
    post(beside[1], 2)
    post(beside[0], 1)
    slots2[z] = total

    @pl.when(z < 7)
    def _():
        pl.semaphore_wait(entered, 3 * (7 - z))
        higher(post_all)

    got2 = slots2.at[pl.ds(0, 23)]
    pltpu.make_async_copy(got2, got2, recv2).wait()
    sums = []
    for i in range(3):
        both = slots2[8 * i : 8 * i + 8].sum(axis=0)
        sums.append(jnp.concatenate([both, pltpu.roll(both, 64, 1)], axis=0))

    blocks = coefs_of(sums, inverse)
    left = weights(blocks, row_of, ((0, (0, 1)), (1, (0, 2))), spread, tile)

    def rows_of(left, start, h):
        right = jnp.concatenate(
            [
                jnp.concatenate([ref[:, c0 + c].reshape(VROWS, 128) for c in range(WIDTH)], axis=1)
                for ref, c0 in ((v, start), (pair.at[h], start - h * HALF))
            ],
            axis=0,
        )
        return jnp.dot(left, right, preferred_element_type=F32)

    sends = [None] * (C // WIDTH)
    for i in range(HALF // WIDTH):
        for h in range(2):
            if i == 0:
                exchange[h].wait_recv()
            start = h * HALF + i * WIDTH
            out = rows_of(left[h], start, h)
            for c in range(WIDTH):
                send[:, start + c] = out[:, c * 128 : c * 128 + 128].astype(BF16).reshape(OUT, 32, 128)
            part = pl.ds(start, WIDTH)
            n = start // WIDTH
            sends[n] = pltpu.make_async_remote_copy(
                send.at[:, part], recv.at[:, part], send3.at[n], recv3.at[n],
                device_id=beside[1 - h], device_id_type=MESH,
            )
            sends[n].start()
    home = weights(blocks, row_of, ((2, (0, 1)), (2, (0, 2))), spread, tile)
    for h in range(2):
        for start in range(h * HALF, (h + 1) * HALF, WIDTH):
            out = rows_of(home[h], start, h)
            for c in range(WIDTH):
                o_ref[:, start + c] = out[:, c * 128 : c * 128 + 128].reshape(OUT, 32, 128)

    for h in range(2):
        exchange[h].wait_send()
    pltpu.make_async_copy(got, got, send1).wait()
    pltpu.make_async_copy(got2, got2, send2).wait()
    for i, copy in enumerate(sends):
        copy.wait_recv()
        part = slice(i * WIDTH, (i + 1) * WIDTH)
        o_ref[:, part] += recv[:, part].astype(F32)
    for copy in sends:
        copy.wait_send()


def on_device(vectors, sources, eigenvalues):
    def tiles(x):
        n = x.shape[0]
        return x.reshape(n, 2, C, T, 128).transpose(0, 2, 3, 1, 4).reshape(n, C, 2 * T, 128)

    dma = pltpu.SemaphoreType.DMA
    out = pl.pallas_call(
        kernel,
        out_shape=pltpu.VMEM((OUT, C, 2 * T, 128), F32),
        in_specs=[
            pl.BlockSpec(memory_space=pltpu.HBM),
            pl.BlockSpec(memory_space=pltpu.HBM),
            pl.BlockSpec(memory_space=pltpu.HBM),
        ],
        out_specs=pl.BlockSpec(memory_space=pltpu.VMEM),
        scratch_shapes=[
            pltpu.VMEM((K, C, 2 * T, 128), BF16),
            pltpu.VMEM((S, C, 2 * T, 128), BF16),
            pltpu.SMEM((32,), F32),
            pltpu.VMEM((32, VROWS), F32),
            pltpu.VMEM((3 * VROWS, 128), BF16),
            pltpu.VMEM((128, VROWS), BF16),
            pltpu.VMEM((3 * OUT, 8, 128), F32),
            pltpu.VMEM((3, 8, 128), F32),
            pltpu.VMEM((2, K, HALF, 2 * T, 128), BF16),
            pltpu.VMEM((4, 128), F32),
            pltpu.VMEM((16, 4, 128), F32),
            pltpu.VMEM((4, 128), F32),
            pltpu.VMEM((24, 4, 128), F32),
            pltpu.VMEM((OUT, C, 2 * T, 128), BF16),
            pltpu.VMEM((OUT, C, 2 * T, 128), BF16),
            dma((3,)), dma((2,)), dma((2,)), dma, dma, dma, dma, dma((C // WIDTH,)), dma((C // WIDTH,)),
            pltpu.SemaphoreType.REGULAR,
        ],
        compiler_params=pltpu.CompilerParams(
            collective_id=0, has_side_effects=True, vmem_limit_bytes=60 * 2**20
        ),
        name="deflate",
    )(tiles(vectors), tiles(sources), eigenvalues)
    return out.reshape(OUT, C, T, 2, 128).transpose(0, 3, 1, 2, 4).reshape(OUT, 2, C, T * 128)


def solution(mesh):
    in_specs = (P("mode", None, None, ("tm", "gz")), P(None, None, None, ("tm", "gz")), P())
    out_specs = P("mode", None, None, ("tm", "gz"))
    return jax.shard_map(
        on_device, mesh=mesh, in_specs=in_specs, out_specs=out_specs, check_vma=False
    )
```
